512 devices in a mesh: dp: 64 (over y_hi, z, core), tensor: 8 (over x, y_lo).
Axes of the slice: x: 4, y: 4 (y_hi: 2, y_lo: 2; y = y_hi * 2 + y_lo), z: 16, core: 2. Of those that a mesh axis runs over, the one named last changes fastest.
Arguments:
- activations: bfloat16 [32768, 7168], P('dp', 'tensor'), may hold values from -6 to 6
- out_grad: bfloat16 [32768, 9216], P('dp', 'tensor'), may hold values from -1 to 1
- projector: float32 [7168, 512], P('tensor'), may hold values from -0.0625 to 0.0625
- moment_one: float32 [512, 9216], P(None, ('tensor', 'dp')), may hold values from -4 to 4
- moment_two: float32 [512, 9216], P(None, ('tensor', 'dp')), may hold values from 0.001 to 0.05
Outputs:
- update: bfloat16 [7168, 9216], P('dp', 'tensor')
- moment_first: float32 [512, 9216], P(None, ('tensor', 'dp'))
- moment_second: float32 [512, 9216], P(None, ('tensor', 'dp'))
The draws below stay inside these ranges and needn't reach their ends.
All inputs are finite; a program needn't handle non-finite values.
Results may differ from the reference program's by a relative error of at most 0.0057.
Values may be sent and summed in bfloat16 or wider, within the bound.
No kernel may reach another device: no remote copies, remote signals or barrier semaphores. Data moves between devices by JAX's collectives and lax.ppermute only.
A program may use at most 64 MiB of HBM per device.

```python
import math
import jax
import jax.numpy as jnp
from jax import lax

D = 7168
FF = 9216
R = 512
TOKENS = 32768


def draw_out_grad(key, part):
    key = jax.random.fold_in(key, 7)
    scale_base = jnp.minimum(3.0 / jnp.sqrt(jnp.float32(TOKENS)), jnp.float32(1.0 / 6.0))
    values = jax.random.truncated_normal(key, -6.0, 6.0, (TOKENS, FF), jnp.float32)
    return (values * scale_base).astype(jnp.bfloat16)


def block_levels(key, extent, shards, smallest, high):
    gain, own = 1.0, jax.random.fold_in(key, 6)
    for dim, shards_of in shards:
        heights = jnp.exp(jax.random.uniform(jax.random.fold_in(own, dim), (shards_of,), jnp.float32, smallest / len(shards), high / len(shards)))
        gain = gain * jnp.repeat(heights, extent[dim] // shards_of).reshape([-1 if axis == dim else 1 for axis in range(len(extent))])
    return gain


def normal_values(own_key, extent, deviation, bound, cuts=(), kind=jnp.bfloat16):
    values = deviation * jax.random.normal(own_key, extent, jnp.float32)
    if cuts:
        values = values * block_levels(own_key, extent, cuts, -0.22, 0.18)
    return jnp.clip(values, -bound, bound).astype(kind)


def setup_inputs(seed: int = 0) -> dict:
    key_list = jax.random.split(jax.random.key(seed), 6)
    return {
        "activations": normal_values(key_list[0], (TOKENS, D), 1.0, 6.0, ((0, 64), (1, 8))),
        "out_grad": draw_out_grad(jax.random.fold_in(key_list[5], 71), 0),
        "projector": normal_values(key_list[2], (D, R), D ** -0.5, 0.0625, ((0, 8),), jnp.float32),
        "moment_one": normal_values(key_list[3], (R, FF), 0.3, 4.0, ((1, 512),), jnp.float32),
        "moment_two": jnp.clip(jnp.exp(math.log(0.05) - 3.912023 * jax.random.uniform(key_list[4], (R, FF), jnp.float32) ** block_levels(key_list[4], (R, FF), ((1, 512),), -0.2, 0.2)), 0.001, 0.05),
    }


beta_first = 0.9
beta_second = 0.999
bias_first = 0.999973438601112
bias_second = 0.095207852886291
adam_eps = 1e-08

def reference(activations, out_grad, projector, moment_one, moment_two):
    projected = jnp.dot(activations.astype(jnp.float32), projector, precision=lax.Precision.HIGHEST).astype(jnp.bfloat16)
    gradient = lax.dot_general(projected, out_grad, (((0,), (0,)), ((), ())), preferred_element_type=jnp.float32)
    moment_first = beta_first * moment_one + (1.0 - beta_first) * gradient
    moment_second = beta_second * moment_two + (1.0 - beta_second) * gradient * gradient
    normed = (moment_first / bias_first / (jnp.sqrt(moment_second / bias_second) + adam_eps)).astype(jnp.bfloat16)
    update = jnp.dot(projector, normed.astype(jnp.float32), precision=lax.Precision.HIGHEST).astype(jnp.bfloat16)
    return (update, moment_first, moment_second)
```

```python
import jax
import jax.numpy as jnp
from jax import lax
from jax.experimental import pallas as pl
from jax.experimental.pallas import tpu as pltpu
from jax.sharding import Mesh, PartitionSpec as P

beta_first = 0.9
beta_second = 0.999
bias_first = 0.999973438601112
bias_second = 0.095207852886291
adam_eps = 1e-08

AXES = ("y_hi", "z_far", "z_near", "core", "x", "y_lo")
SIZES = (2, 8, 2, 2, 4, 2)
DP = AXES[:4]
TENSOR = AXES[4:]
NEAR = ("y_hi", "z_near")
bf16, f32 = jnp.bfloat16, jnp.float32
CORE_SWAP = [(0, 1), (1, 0)]


def swap_cores(value):
    return lax.ppermute(value, "core", CORE_SWAP)


def spread(value, axes, count):
    copies = jnp.broadcast_to(value[None], (count,) + value.shape)
    return lax.all_to_all(copies, axes, 0, 0)


def halves(value, core, axis):
    size = value.shape[axis] // 2
    own = lax.dynamic_slice_in_dim(value, core * size, size, axis)
    other = lax.dynamic_slice_in_dim(value, (1 - core) * size, size, axis)
    return own, other


def in_order(own, other, place, axis):
    return jnp.where(
        place == 0,
        jnp.concatenate([own, other], axis),
        jnp.concatenate([other, own], axis),
    )


def adam(decayed_one, decayed_two, gradient):
    first = decayed_one + (1.0 - beta_first) * gradient
    second = decayed_two + (1.0 - beta_second) * gradient * gradient
    return first, second


def in_two(value):
    high = value.astype(bf16)
    return high, (value - high.astype(f32)).astype(bf16)


def contract(left, right, left_dim, right_dim):
    return lax.dot_general(
        left, right, (((left_dim,), (right_dim,)), ((), ())), preferred_element_type=f32
    )


def project_kernel(start_ref, activations_ref, projector_ref, parts_ref):
    high, low = in_two(projector_ref[...])
    left = activations_ref[...]
    sums = (contract(left, high, 1, 0) + contract(left, low, 1, 0)).astype(bf16)
    few = left.shape[0] // 8
    rows = projector_ref.shape[0] // 8
    start = pl.multiple_of(start_ref[0], 8)
    basis = projector_ref[pl.ds(start, rows), :].astype(bf16)
    for peer in range(8):
        parts_ref[peer, :few, :] = sums[peer * few : (peer + 1) * few]
        if peer < 7:
            parts_ref[peer, few:, :] = basis[peer * 16 : (peer + 1) * 16]
        else:
            parts_ref[peer, few:, :] = jnp.zeros((16, basis.shape[1]), bf16)


def project(activations, projector, row_start):
    tokens, features = activations.shape
    rank = projector.shape[1]
    wide = rank // 2
    few = tokens // 8 + 16
    return pl.pallas_call(
        project_kernel,
        out_shape=jax.ShapeDtypeStruct((8, few, rank), bf16),
        grid_spec=pltpu.PrefetchScalarGridSpec(
            num_scalar_prefetch=1,
            grid=(2,),
            in_specs=[
                pl.BlockSpec((tokens, features), lambda i, _: (0, 0)),
                pl.BlockSpec((features, wide), lambda i, _: (0, i)),
            ],
            out_specs=pl.BlockSpec((8, few, wide), lambda i, _: (0, 0, i)),
        ),
        compiler_params=pltpu.CompilerParams(vmem_limit_bytes=58 << 20),
        name="project",
    )(row_start.reshape(1).astype(jnp.int32), activations, projector)


def gradient_kernel(own_ref, other_ref, both_ref, out_ref, left, total):
    step = pl.program_id(0)
    few = both_ref.shape[2] - 16
    tokens = own_ref.shape[0]
    wide = own_ref.shape[1]

    @pl.when(step == 0)
    def _():
        for side in range(2):
            for peer in range(8):
                left[side, peer * few : (peer + 1) * few, :] = both_ref[peer, side, :few, :]

    sums = contract(own_ref[...], left[0], 0, 0) + contract(other_ref[...], left[1], 0, 0)
    total[pl.ds(pl.multiple_of(step * wide, wide), wide), :] = sums

    @pl.when(step == pl.num_programs(0) - 1)
    def _():
        places, each = out_ref.shape[1], out_ref.shape[2] // 2
        for y_hi in range(2):
            for z_near in range(2):
                for z_far in range(places):
                    at = ((y_hi * places + z_far) * 2 + z_near) * each
                    block = total[at : at + each, :]
                    block = jnp.concatenate([block[:, :128], block[:, 128:]], 0)
                    out_ref[y_hi * 2 + z_near, z_far] = block.astype(bf16)


def gradient_parts(own, other, both):
    tokens, width = own.shape
    half = both.shape[3]
    steps = 3
    wide = width // steps
    out = (4, 8, width // 16, half // 2)
    return pl.pallas_call(
        gradient_kernel,
        out_shape=jax.ShapeDtypeStruct(out, bf16),
        grid=(steps,),
        in_specs=[
            pl.BlockSpec((tokens, wide), lambda i: (0, i)),
            pl.BlockSpec((tokens, wide), lambda i: (0, i)),
            pl.BlockSpec(both.shape, lambda i: (0, 0, 0, 0)),
        ],
        out_specs=pl.BlockSpec(out, lambda i: (0, 0, 0, 0)),
        scratch_shapes=[
            pltpu.VMEM((2, tokens, half), bf16),
            pltpu.VMEM((width, half), f32),
        ],
        compiler_params=pltpu.CompilerParams(vmem_limit_bytes=40 << 20),
        name="gradient",
    )(own, other, both)


def step_kernel(far_ref, moments_ref, normed_ref, total_ref):
    total = jnp.sum(far_ref[...].astype(f32), axis=0)
    each = total.shape[0] // 2
    for part in range(2):
        total_ref[part] = total[part * each : (part + 1) * each]
    decayed = [jnp.concatenate([moments_ref[i, 0], moments_ref[i, 1]], 0) for i in range(2)]
    first, second = adam(decayed[0], decayed[1], total)
    normed = first / bias_first / (jnp.sqrt(second / bias_second) + adam_eps)
    normed = normed.astype(bf16)
    for place in range(8):
        normed_ref[place] = normed


def step(far, moments):
    return pl.pallas_call(
        step_kernel,
        out_shape=(
            jax.ShapeDtypeStruct(far.shape, bf16),
            jax.ShapeDtypeStruct(moments.shape[1:], f32),
        ),
        name="step",
    )(far, moments)


def local(activations, out_grad, projector, moment_one, moment_two):
    y_hi = lax.axis_index("y_hi")
    z_far = lax.axis_index("z_far")
    z_near = lax.axis_index("z_near")
    core = lax.axis_index("core")
    tokens, rank, width = out_grad.shape[0], projector.shape[1], out_grad.shape[1]
    half = rank // 2
    each = width // 32
    few = tokens // 8
    rows = projector.shape[0] // 8

    row_start = ((z_far % 2) * 4 + z_near * 2 + core) * rows
    parts = project(activations, projector, row_start)
    parts, out_grad, moment_one, moment_two = lax.optimization_barrier(
        (parts, out_grad, moment_one, moment_two)
    )
    parts = lax.all_to_all(parts, TENSOR, 0, 0)

    grad_other = swap_cores(out_grad)
    moments = jnp.stack([beta_first * moment_one.T, beta_second * moment_two.T])
    keep, send = halves(moments.reshape(2, each // 2, 4, 128).transpose(0, 2, 1, 3), core, 1)
    moments = in_order(keep, swap_cores(send), core, 2)
    summed = parts[:, :few].astype(f32).sum(0).astype(bf16)
    row_part = lax.dynamic_index_in_dim(parts[:, few:], y_hi * 4 + z_far // 2, 0, keepdims=False)
    summed, moments = lax.optimization_barrier((summed, moments))

    own, other = halves(summed, core, 1)
    both = jnp.stack([own, swap_cores(other)])
    both = jnp.concatenate([both, jnp.stack(halves(row_part, core, 1))], 1)
    both = spread(both, TENSOR, 8)
    row_basis = both[:7, :, few:]

    near = lax.all_to_all(gradient_parts(out_grad, grad_other, both), NEAR, 0, 0)
    near = near.astype(f32).sum(0).astype(bf16)
    far = lax.all_to_all(near, "z_far", 0, 0)
    normed, total = step(far, moments)
    normed = lax.all_to_all(normed, "z_far", 0, 0)

    back_own, back_other = halves(total, core, 1)
    own_gradient = in_order(back_own, swap_cores(back_other), core, 0)
    normed, own_gradient = lax.optimization_barrier((normed, own_gradient))
    own_gradient = own_gradient.transpose(1, 0, 2).reshape(each // 2, rank).T
    moment_first, moment_second = adam(
        beta_first * moment_one, beta_second * moment_two, own_gradient
    )

    normed_own = spread(normed, NEAR, 4).reshape(2, 2, 8, 2, each, 128)
    normed_own = normed_own.transpose(0, 2, 1, 4, 3, 5).reshape(width, half)
    normed_other = swap_cores(normed_own)
    update = 0.0
    for side, half_step in enumerate((normed_own, normed_other)):
        update = update + contract(row_basis[:, side].reshape(rows, half), half_step, 1, 1)
    return (update.astype(bf16), moment_first, moment_second)


def solution(mesh):
    fine = Mesh(mesh.devices.reshape(SIZES), AXES)
    placed = (
        P(DP, TENSOR),
        P(DP, TENSOR),
        P(TENSOR, None),
        P(None, TENSOR + DP),
        P(None, TENSOR + DP),
    )
    return jax.shard_map(
        local,
        mesh=fine,
        in_specs=placed,
        out_specs=(P(DP, TENSOR), P(None, TENSOR + DP), P(None, TENSOR + DP)),
        check_vma=False,
    )
```

```python
import jax
import jax.numpy as jnp
from jax import lax
from jax.experimental import pallas as pl
from jax.experimental.pallas import tpu as pltpu
from jax.sharding import Mesh, PartitionSpec as P

beta_first = 0.9
beta_second = 0.999
bias_first = 0.999973438601112
bias_second = 0.095207852886291
adam_eps = 1e-08

AXES = ("y_hi", "z3", "z2", "z1", "z0", "core", "x", "y_lo")
SIZES = (2, 2, 2, 2, 2, 2, 4, 2)
DP = AXES[:6]
TENSOR = AXES[6:]
SUMMING = ("x", "y_lo")
NEAR = ("y_hi", "z0")
FAR = ("z1", "z2", "z3")
bf16, f32 = jnp.bfloat16, jnp.float32
CORE_SWAP = [(0, 1), (1, 0)]


def place_in(axes, coords):
    index = 0
    for axis in axes:
        index = index * SIZES[AXES.index(axis)] + coords[axis]
    return index


def swap_cores(value):
    return lax.ppermute(value, "core", CORE_SWAP)


def spread(value, axes, count):
    copies = jnp.broadcast_to(value[None], (count,) + value.shape)
    return lax.all_to_all(copies, axes, 0, 0)


def halves(value, core, axis):
    size = value.shape[axis] // 2
    own = lax.dynamic_slice_in_dim(value, core * size, size, axis)
    other = lax.dynamic_slice_in_dim(value, (1 - core) * size, size, axis)
    return own, other


def in_order(own, other, place, axis):
    return jnp.where(
        place == 0,
        jnp.concatenate([own, other], axis),
        jnp.concatenate([other, own], axis),
    )


def adam(decayed_one, decayed_two, gradient):
    first = decayed_one + (1.0 - beta_first) * gradient
    second = decayed_two + (1.0 - beta_second) * gradient * gradient
    return first, second


def in_two(value):
    high = value.astype(bf16)
    return high, (value - high.astype(f32)).astype(bf16)


def contract(left, right, left_dim, right_dim):
    return lax.dot_general(
        left, right, (((left_dim,), (right_dim,)), ((), ())), preferred_element_type=f32
    )


def project_kernel(start_ref, activations_ref, projector_ref, parts_ref):
    high, low = in_two(projector_ref[...])
    left = activations_ref[...]
    sums = (contract(left, high, 1, 0) + contract(left, low, 1, 0)).astype(bf16)
    few = left.shape[0] // 8
    rows = projector_ref.shape[0] // 8
    start = pl.multiple_of(start_ref[0], 8)
    basis = projector_ref[pl.ds(start, rows), :].astype(bf16)
    for peer in range(8):
        parts_ref[peer, :few, :] = sums[peer * few : (peer + 1) * few]
        if peer < 7:
            parts_ref[peer, few:, :] = basis[peer * 16 : (peer + 1) * 16]
        else:
            parts_ref[peer, few:, :] = jnp.zeros((16, basis.shape[1]), bf16)


def project(activations, projector, row_start):
    tokens, features = activations.shape
    rank = projector.shape[1]
    wide = rank // 2
    few = tokens // 8 + 16
    return pl.pallas_call(
        project_kernel,
        out_shape=jax.ShapeDtypeStruct((8, few, rank), bf16),
        grid_spec=pltpu.PrefetchScalarGridSpec(
            num_scalar_prefetch=1,
            grid=(2,),
            in_specs=[
                pl.BlockSpec((tokens, features), lambda i, _: (0, 0)),
                pl.BlockSpec((features, wide), lambda i, _: (0, i)),
            ],
            out_specs=pl.BlockSpec((8, few, wide), lambda i, _: (0, 0, i)),
        ),
        compiler_params=pltpu.CompilerParams(vmem_limit_bytes=58 << 20),
        name="project",
    )(row_start.reshape(1).astype(jnp.int32), activations, projector)


def gradient_kernel(own_ref, other_ref, both_ref, out_ref, left, total):
    step = pl.program_id(0)
    few = both_ref.shape[1] - 16
    half = left.shape[2]
    tokens = own_ref.shape[0]
    wide = own_ref.shape[1]

    @pl.when(step == 0)
    def _():
        for side in range(2):
            for peer in range(8):
                left[side, peer * few : (peer + 1) * few, :] = both_ref[
                    peer, :few, side * half : (side + 1) * half
                ]

    sums = contract(own_ref[...], left[0], 0, 0) + contract(other_ref[...], left[1], 0, 0)
    total[pl.ds(pl.multiple_of(step * wide, wide), wide), :] = sums

    @pl.when(step == pl.num_programs(0) - 1)
    def _():
        each = out_ref.shape[2] // 2
        for index in range(total.shape[0] // each):
            coords = {axis: index >> (4 - bit) & 1 for bit, axis in enumerate(AXES[:5])}
            block = total[index * each : (index + 1) * each, :]
            block = jnp.concatenate([block[:, :128], block[:, 128:]], 0)
            out_ref[place_in(NEAR, coords), place_in(FAR, coords)] = block.astype(bf16)


def gradient_parts(own, other, both):
    tokens, width = own.shape
    half = both.shape[2] // 2
    steps = 3
    wide = width // steps
    out = (4, 8, width // 16, half // 2)
    return pl.pallas_call(
        gradient_kernel,
        out_shape=jax.ShapeDtypeStruct(out, bf16),
        grid=(steps,),
        in_specs=[
            pl.BlockSpec((tokens, wide), lambda i: (0, i)),
            pl.BlockSpec((tokens, wide), lambda i: (0, i)),
            pl.BlockSpec(both.shape, lambda i: (0, 0, 0)),
        ],
        out_specs=pl.BlockSpec(out, lambda i: (0, 0, 0, 0)),
        scratch_shapes=[
            pltpu.VMEM((2, tokens, half), bf16),
            pltpu.VMEM((width, half), f32),
        ],
        compiler_params=pltpu.CompilerParams(vmem_limit_bytes=40 << 20),
        name="gradient",
    )(own, other, both)


def step_kernel(far_ref, moments_ref, normed_ref, total_ref):
    total = jnp.sum(far_ref[...].astype(f32), axis=0)
    each = total.shape[0] // 2
    for part in range(2):
        total_ref[part] = total[part * each : (part + 1) * each]
    decayed = [jnp.concatenate([moments_ref[i, 0], moments_ref[i, 1]], 0) for i in range(2)]
    first, second = adam(decayed[0], decayed[1], total)
    normed = first / bias_first / (jnp.sqrt(second / bias_second) + adam_eps)
    normed = normed.astype(bf16)
    for place in range(8):
        normed_ref[place] = normed


def step(far, moments):
    return pl.pallas_call(
        step_kernel,
        out_shape=(
            jax.ShapeDtypeStruct(far.shape, bf16),
            jax.ShapeDtypeStruct(moments.shape[1:], f32),
        ),
        name="step",
    )(far, moments)


def local(activations, out_grad, projector, moment_one, moment_two):
    y_hi, z3, z2, z1, z0, core = (lax.axis_index(axis) for axis in DP)
    tokens, rank, width = out_grad.shape[0], projector.shape[1], out_grad.shape[1]
    half = rank // 2
    each = width // 32
    few = tokens // 8
    rows = projector.shape[0] // 8

    row_start = (z1 * 4 + z0 * 2 + core) * rows
    parts = project(activations, projector, row_start)
    parts, out_grad, moment_one, moment_two = lax.optimization_barrier(
        (parts, out_grad, moment_one, moment_two)
    )
    parts = lax.all_to_all(parts, SUMMING, 0, 0)

    grad_other = swap_cores(out_grad)
    moments = jnp.stack([beta_first * moment_one.T, beta_second * moment_two.T])
    keep, send = halves(moments.reshape(2, each // 2, 4, 128).transpose(0, 2, 1, 3), core, 1)
    moments = in_order(keep, swap_cores(send), core, 2)
    summed = parts[:, :few].astype(f32).sum(0).astype(bf16)
    holder = place_in(SUMMING, {"x": y_hi * 2 + z3, "y_lo": z2})
    row_part = lax.dynamic_index_in_dim(parts[:, few:], holder, 0, keepdims=False)
    summed, moments = lax.optimization_barrier((summed, moments))

    own, other = halves(summed, core, 1)
    both = jnp.concatenate([own, swap_cores(other)], 1)
    both = jnp.concatenate([both, jnp.concatenate(halves(row_part, core, 1), 1)], 0)
    both = spread(both, SUMMING, 8)
    row_basis = both[:7, few:].reshape(rows, rank)

    near = gradient_parts(out_grad, grad_other, both).reshape(4, 16 * each, 128)
    near = lax.all_to_all(near, NEAR, 0, 0).astype(f32).sum(0).astype(bf16)
    far = lax.all_to_all(near.reshape(8, 2 * each, 128), FAR, 0, 0)
    normed, total = step(far, moments)
    normed = lax.all_to_all(normed, FAR, 0, 0)

    back_own, back_other = halves(total, core, 1)
    own_gradient = in_order(back_own, swap_cores(back_other), core, 0)
    normed, own_gradient = lax.optimization_barrier((normed, own_gradient))
    own_gradient = own_gradient.transpose(1, 0, 2).reshape(each // 2, rank).T
    moment_first, moment_second = adam(
        beta_first * moment_one, beta_second * moment_two, own_gradient
    )

    normed = spread(normed.reshape(16 * each, 128), NEAR, 4)
    normed = normed.reshape((2,) * 6 + (each, 128))
    order = [(NEAR + FAR).index(axis) for axis in AXES[:5]]
    normed_own = normed.transpose(*order, 6, 5, 7).reshape(width, half)
    normed_other = swap_cores(normed_own)
    update = 0.0
    for side, half_step in enumerate((normed_own, normed_other)):
        left = row_basis[:, side * half : (side + 1) * half]
        update = update + contract(left, half_step, 1, 1)
    return (update.astype(bf16), moment_first, moment_second)


def solution(mesh):
    fine = Mesh(mesh.devices.reshape(SIZES), AXES)
    placed = (
        P(DP, TENSOR),
        P(DP, TENSOR),
        P(TENSOR, None),
        P(None, TENSOR + DP),
        P(None, TENSOR + DP),
    )
    return jax.shard_map(
        local,
        mesh=fine,
        in_specs=placed,
        out_specs=(P(DP, TENSOR), P(None, TENSOR + DP), P(None, TENSOR + DP)),
        check_vma=False,
    )
```

```python
import jax
import jax.numpy as jnp
from jax import lax
from jax.experimental import pallas as pl
from jax.experimental.pallas import tpu as pltpu
from jax.sharding import Mesh, PartitionSpec as P

beta_first = 0.9
beta_second = 0.999
bias_first = 0.999973438601112
bias_second = 0.095207852886291
adam_eps = 1e-08

AXES = ("y_hi", "z3", "z2", "z1", "z0", "core", "x", "y_lo")
SIZES = (2, 2, 2, 2, 2, 2, 4, 2)
DP = AXES[:6]
TENSOR = AXES[6:]
SUMMING = ("x", "y_lo")
NEAR = ("y_hi", "z0")
FAR = ("z1", "z2", "z3")
bf16, f32 = jnp.bfloat16, jnp.float32
CORE_SWAP = [(0, 1), (1, 0)]


def place_in(axes, coords):
    index = 0
    for axis in axes:
        index = index * SIZES[AXES.index(axis)] + coords[axis]
    return index


def swap_cores(value):
    return lax.ppermute(value, "core", CORE_SWAP)


def spread(value, axes, count):
    copies = jnp.broadcast_to(value[None], (count,) + value.shape)
    return lax.all_to_all(copies, axes, 0, 0)


def halves(value, core, axis):
    size = value.shape[axis] // 2
    own = lax.dynamic_slice_in_dim(value, core * size, size, axis)
    other = lax.dynamic_slice_in_dim(value, (1 - core) * size, size, axis)
    return own, other


def in_order(own, other, place, axis):
    return jnp.where(
        place == 0,
        jnp.concatenate([own, other], axis),
        jnp.concatenate([other, own], axis),
    )


def adam(decayed_one, decayed_two, gradient):
    first = decayed_one + (1.0 - beta_first) * gradient
    second = decayed_two + (1.0 - beta_second) * gradient * gradient
    return first, second


def in_two(value):
    high = value.astype(bf16)
    return high, (value - high.astype(f32)).astype(bf16)


def contract(left, right, left_dim, right_dim):
    return lax.dot_general(
        left, right, (((left_dim,), (right_dim,)), ((), ())), preferred_element_type=f32
    )


def project_kernel(start_ref, activations_ref, projector_ref, parts_ref):
    high, low = in_two(projector_ref[...])
    left = activations_ref[...]
    sums = (contract(left, high, 1, 0) + contract(left, low, 1, 0)).astype(bf16)
    few = left.shape[0] // 8
    rows = projector_ref.shape[0] // 8
    start = pl.multiple_of(start_ref[0], 8)
    basis = projector_ref[pl.ds(start, rows), :].astype(bf16)
    for peer in range(8):
        parts_ref[peer, :few, :] = sums[peer * few : (peer + 1) * few]
        if peer < 7:
            parts_ref[peer, few:, :] = basis[peer * 16 : (peer + 1) * 16]
        else:
            parts_ref[peer, few:, :] = jnp.zeros((16, basis.shape[1]), bf16)


def project(activations, projector, row_start):
    tokens, features = activations.shape
    rank = projector.shape[1]
    wide = rank // 2
    few = tokens // 8 + 16
    return pl.pallas_call(
        project_kernel,
        out_shape=jax.ShapeDtypeStruct((8, few, rank), bf16),
        grid_spec=pltpu.PrefetchScalarGridSpec(
            num_scalar_prefetch=1,
            grid=(2,),
            in_specs=[
                pl.BlockSpec((tokens, features), lambda i, _: (0, 0)),
                pl.BlockSpec((features, wide), lambda i, _: (0, i)),
            ],
            out_specs=pl.BlockSpec((8, few, wide), lambda i, _: (0, 0, i)),
        ),
        compiler_params=pltpu.CompilerParams(vmem_limit_bytes=58 << 20),
        name="project",
    )(row_start.reshape(1).astype(jnp.int32), activations, projector)


def gradient_kernel(own_ref, other_ref, both_ref, out_ref, left, total):
    few = both_ref.shape[1] - 16
    half = left.shape[2]
    wide = total.shape[0] // 3
    for side in range(2):
        for peer in range(8):
            left[side, peer * few : (peer + 1) * few, :] = both_ref[
                peer, :few, side * half : (side + 1) * half
            ]
    for at in range(0, total.shape[0], wide):
        sums = contract(own_ref[:, at : at + wide], left[0], 0, 0)
        total[at : at + wide, :] = sums + contract(other_ref[:, at : at + wide], left[1], 0, 0)
    each = out_ref.shape[2] // 2
    for index in range(total.shape[0] // each):
        coords = {axis: index >> (4 - bit) & 1 for bit, axis in enumerate(AXES[:5])}
        block = total[index * each : (index + 1) * each, :]
        block = jnp.concatenate([block[:, :128], block[:, 128:]], 0)
        out_ref[place_in(NEAR, coords), place_in(FAR, coords)] = block.astype(bf16)


def gradient_parts(own, other, both):
    tokens, width = own.shape
    half = both.shape[2] // 2
    return pl.pallas_call(
        gradient_kernel,
        out_shape=jax.ShapeDtypeStruct((4, 8, width // 16, half // 2), bf16),
        in_specs=[pl.BlockSpec(memory_space=pltpu.VMEM)] * 3,
        out_specs=pl.BlockSpec(memory_space=pltpu.VMEM),
        scratch_shapes=[
            pltpu.VMEM((2, tokens, half), bf16),
            pltpu.VMEM((width, half), f32),
        ],
        compiler_params=pltpu.CompilerParams(vmem_limit_bytes=40 << 20),
        name="gradient",
    )(own, other, both)


def step_kernel(far_ref, moments_ref, normed_ref, total_ref):
    total = jnp.sum(far_ref[...].astype(f32), axis=0)
    each = total.shape[0] // 2
    for part in range(2):
        total_ref[part] = total[part * each : (part + 1) * each]
    decayed = [jnp.concatenate([moments_ref[i, 0], moments_ref[i, 1]], 0) for i in range(2)]
    first, second = adam(decayed[0], decayed[1], total)
    normed = first / bias_first / (jnp.sqrt(second / bias_second) + adam_eps)
    normed = normed.astype(bf16)
    for place in range(8):
        normed_ref[place] = normed


def step(far, moments):
    return pl.pallas_call(
        step_kernel,
        out_shape=(
            jax.ShapeDtypeStruct(far.shape, bf16),
            jax.ShapeDtypeStruct(moments.shape[1:], f32),
        ),
        in_specs=[pl.BlockSpec(memory_space=pltpu.VMEM)] * 2,
        name="step",
    )(far, moments)


def local(activations, out_grad, projector, moment_one, moment_two):
    y_hi, z3, z2, z1, z0, core = (lax.axis_index(axis) for axis in DP)
    tokens, rank, width = out_grad.shape[0], projector.shape[1], out_grad.shape[1]
    half = rank // 2
    each = width // 32
    few = tokens // 8
    rows = projector.shape[0] // 8

    row_start = (z1 * 4 + z0 * 2 + core) * rows
    parts = project(activations, projector, row_start)
    parts, out_grad, moment_one, moment_two = lax.optimization_barrier(
        (parts, out_grad, moment_one, moment_two)
    )
    parts = lax.all_to_all(parts, SUMMING, 0, 0)

    grad_other = swap_cores(out_grad)
    moments = jnp.stack([beta_first * moment_one.T, beta_second * moment_two.T])
    keep, send = halves(moments.reshape(2, each // 2, 4, 128).transpose(0, 2, 1, 3), core, 1)
    moments = in_order(keep, swap_cores(send), core, 2)
    summed = parts[:, :few].astype(f32).sum(0).astype(bf16)
    holder = place_in(SUMMING, {"x": y_hi * 2 + z3, "y_lo": z2})
    row_part = lax.dynamic_index_in_dim(parts[:, few:], holder, 0, keepdims=False)
    summed, moments = lax.optimization_barrier((summed, moments))

    own, other = halves(summed, core, 1)
    both = jnp.concatenate([own, swap_cores(other)], 1)
    both = jnp.concatenate([both, jnp.concatenate(halves(row_part, core, 1), 1)], 0)
    both = spread(both, SUMMING, 8)
    row_basis = both[:7, few:].reshape(rows, rank)

    near = gradient_parts(out_grad, grad_other, both).reshape(4, 16 * each, 128)
    near = lax.all_to_all(near, NEAR, 0, 0).astype(f32).sum(0).astype(bf16)
    far = lax.all_to_all(near.reshape(8, 2 * each, 128), FAR, 0, 0)
    normed, total = step(far, moments)
    normed = lax.all_to_all(normed, FAR, 0, 0)

    back_own, back_other = halves(total, core, 1)
    own_gradient = in_order(back_own, swap_cores(back_other), core, 0)
    normed, own_gradient = lax.optimization_barrier((normed, own_gradient))
    own_gradient = own_gradient.transpose(1, 0, 2).reshape(each // 2, rank).T
    moment_first, moment_second = adam(
        beta_first * moment_one, beta_second * moment_two, own_gradient
    )

    normed = spread(normed.reshape(16 * each, 128), NEAR, 4)
    normed = normed.reshape((2,) * 6 + (each, 128))
    order = [(NEAR + FAR).index(axis) for axis in AXES[:5]]
    normed_own = normed.transpose(*order, 6, 5, 7).reshape(width, half)
    normed_other = swap_cores(normed_own)
    update = 0.0
    for side, half_step in enumerate((normed_own, normed_other)):
        left = row_basis[:, side * half : (side + 1) * half]
        update = update + contract(left, half_step, 1, 1)
    return (update.astype(bf16), moment_first, moment_second)


def solution(mesh):
    fine = Mesh(mesh.devices.reshape(SIZES), AXES)
    placed = (
        P(DP, TENSOR),
        P(DP, TENSOR),
        P(TENSOR, None),
        P(None, TENSOR + DP),
        P(None, TENSOR + DP),
    )
    return jax.shard_map(
        local,
        mesh=fine,
        in_specs=placed,
        out_specs=(P(DP, TENSOR), P(None, TENSOR + DP), P(None, TENSOR + DP)),
        check_vma=False,
    )
```

```python
import jax
import jax.numpy as jnp
from jax import lax
from jax.experimental import pallas as pl
from jax.experimental.pallas import tpu as pltpu
from jax.sharding import Mesh, PartitionSpec as P

beta_first = 0.9
beta_second = 0.999
bias_first = 0.999973438601112
bias_second = 0.095207852886291
adam_eps = 1e-08

AXES = ("y_hi", "z3", "z2", "z1", "z0", "core", "x", "y_lo")
SIZES = (2, 2, 2, 2, 2, 2, 4, 2)
DP = AXES[:6]
TENSOR = AXES[6:]
GATHERING = ("x", "y_lo")
SUMMING = ("x", "y_lo", "core")
NEAR = ("y_hi", "z0")
FAR = ("z1", "z2", "z3")
bf16, f32 = jnp.bfloat16, jnp.float32
CORE_SWAP = [(0, 1), (1, 0)]


def place_in(axes, coords):
    index = 0
    for axis in axes:
        index = index * SIZES[AXES.index(axis)] + coords[axis]
    return index


def swap_cores(value):
    return lax.ppermute(value, "core", CORE_SWAP)


def spread(value, axes, count):
    copies = jnp.broadcast_to(value[None], (count,) + value.shape)
    return lax.all_to_all(copies, axes, 0, 0)


def halves(value, core, axis):
    first, second = jnp.split(value, 2, axis)
    return jnp.where(core == 0, first, second), jnp.where(core == 0, second, first)


def in_order(own, other, place, axis):
    return jnp.where(
        place == 0,
        jnp.concatenate([own, other], axis),
        jnp.concatenate([other, own], axis),
    )


def adam(decayed_one, decayed_two, gradient):
    first = decayed_one + (1.0 - beta_first) * gradient
    second = decayed_two + (1.0 - beta_second) * gradient * gradient
    return first, second


def in_two(value):
    high = value.astype(bf16)
    return high, (value - high.astype(f32)).astype(bf16)


def contract(left, right, left_dim, right_dim):
    return lax.dot_general(
        left, right, (((left_dim,), (right_dim,)), ((), ())), preferred_element_type=f32
    )


def project_kernel(place_ref, activations_ref, projector_ref, parts_ref):
    high, low = in_two(projector_ref[...])
    left = activations_ref[...]
    sums = (contract(left, high, 1, 0) + contract(left, low, 1, 0)).astype(bf16)
    few = left.shape[0] // 8
    rows = projector_ref.shape[0] // 8
    for peer in range(8):
        parts_ref[peer, :few, :] = sums[peer * few : (peer + 1) * few]
        eighth = jnp.minimum(peer * 2 + place_ref[0] % 2, rows // 8 - 1) * 8
        start = place_ref[0] // 2 * (2 * rows) + eighth
        basis = [
            projector_ref[pl.ds(pl.multiple_of(start + side * rows, 8), 8), :] for side in range(2)
        ]
        parts_ref[peer, few:, :] = jnp.concatenate(basis, 0).astype(bf16)


def project(activations, projector, place):
    tokens, features = activations.shape
    half = projector.shape[1] // 2
    few = tokens // 8 + 16
    return pl.pallas_call(
        project_kernel,
        out_shape=jax.ShapeDtypeStruct((8, 2 * few, half), bf16),
        grid_spec=pltpu.PrefetchScalarGridSpec(
            num_scalar_prefetch=1,
            grid=(2,),
            in_specs=[
                pl.BlockSpec((tokens, features), lambda i, _: (0, 0)),
                pl.BlockSpec((features, half), lambda i, _: (0, i)),
            ],
            out_specs=pl.BlockSpec((8, few, half), lambda i, _: (0, i, 0)),
        ),
        compiler_params=pltpu.CompilerParams(vmem_limit_bytes=58 << 20),
        name="project",
    )(place.reshape(1).astype(jnp.int32), activations, projector)


def gradient_kernel(core_ref, own_ref, other_ref, both_ref, out_ref, left, total):
    full = both_ref.shape[1] // 2
    few = full - 16
    wide = total.shape[0] // 3
    for side in range(2):
        for peer in range(8):
            left[side, peer * few : (peer + 1) * few, :] = both_ref[
                peer, side * full : side * full + few, :
            ]
    core = core_ref[0]
    for at in range(0, total.shape[0], wide):
        sums = contract(own_ref[:, at : at + wide], left[core], 0, 0)
        total[at : at + wide, :] = sums + contract(other_ref[:, at : at + wide], left[1 - core], 0, 0)
    each = out_ref.shape[2] // 2
    for index in range(total.shape[0] // each):
        coords = {axis: index >> (4 - bit) & 1 for bit, axis in enumerate(AXES[:5])}
        block = total[index * each : (index + 1) * each, :]
        block = jnp.concatenate([block[:, :128], block[:, 128:]], 0)
        out_ref[place_in(NEAR, coords), place_in(FAR, coords)] = block.astype(bf16)


def gradient_parts(own, other, both, core):
    tokens, width = own.shape
    half = both.shape[2]
    return pl.pallas_call(
        gradient_kernel,
        out_shape=jax.ShapeDtypeStruct((4, 8, width // 16, half // 2), bf16),
        in_specs=[pl.BlockSpec(memory_space=pltpu.SMEM)]
        + [pl.BlockSpec(memory_space=pltpu.VMEM)] * 3,
        out_specs=pl.BlockSpec(memory_space=pltpu.VMEM),
        scratch_shapes=[
            pltpu.VMEM((2, tokens, half), bf16),
            pltpu.VMEM((width, half), f32),
        ],
        compiler_params=pltpu.CompilerParams(vmem_limit_bytes=40 << 20),
        name="gradient",
    )(core.reshape(1).astype(jnp.int32), own, other, both)


def step_kernel(far_ref, moments_ref, normed_ref, total_ref):
    total = jnp.sum(far_ref[...].astype(f32), axis=0)
    each = total.shape[0] // 2
    for part in range(2):
        total_ref[part] = total[part * each : (part + 1) * each]
    decayed = [jnp.concatenate([moments_ref[i, 0], moments_ref[i, 1]], 0) for i in range(2)]
    first, second = adam(decayed[0], decayed[1], total)
    normed = first / bias_first / (jnp.sqrt(second / bias_second) + adam_eps)
    normed = normed.astype(bf16)
    for place in range(8):
        normed_ref[place] = normed


def step(far, moments):
    return pl.pallas_call(
        step_kernel,
        out_shape=(
            jax.ShapeDtypeStruct(far.shape, bf16),
            jax.ShapeDtypeStruct(moments.shape[1:], f32),
        ),
        in_specs=[pl.BlockSpec(memory_space=pltpu.VMEM)] * 2,
        compiler_params=pltpu.CompilerParams(vmem_limit_bytes=16 << 20),
        name="step",
    )(far, moments)


def local(activations, out_grad, projector, moment_one, moment_two):
    y_hi, z3, z2, z1, z0, core = (lax.axis_index(axis) for axis in DP)
    tokens, rank, width = out_grad.shape[0], projector.shape[1], out_grad.shape[1]
    half = rank // 2
    each = width // 32
    few = tokens // 8
    rows = projector.shape[0] // 8

    parts = project(activations, projector, z1 * 4 + z0 * 2 + core)
    parts, out_grad, moment_one, moment_two = lax.optimization_barrier(
        (parts, out_grad, moment_one, moment_two)
    )
    parts = lax.all_to_all(parts.reshape(16, few + 16, half), SUMMING, 0, 0)
    parts = parts.reshape(8, 2, few + 16, half)

    grad_other = swap_cores(out_grad)
    moments = jnp.stack([beta_first * moment_one.T, beta_second * moment_two.T])
    keep, send = halves(moments.reshape(2, each // 2, 4, 128).transpose(0, 2, 1, 3), core, 1)
    moments = in_order(keep, swap_cores(send), core, 2)

    summed = parts[:, :, :few].astype(f32).sum(0).astype(bf16)
    holder = place_in(GATHERING, {"x": y_hi * 2 + z3, "y_lo": z2})
    basis = lax.dynamic_index_in_dim(parts[:, :, few:], holder, 0, keepdims=False)
    summed, moments = lax.optimization_barrier((summed, moments))
    both = jnp.concatenate([summed, basis], 1).reshape(2 * few + 32, half)
    both = spread(both, GATHERING, 8)

    near = gradient_parts(out_grad, grad_other, both, core).reshape(4, 16 * each, 128)
    near = lax.all_to_all(near, NEAR, 0, 0).astype(f32).sum(0).astype(bf16)
    far = lax.all_to_all(near.reshape(8, 2 * each, 128), FAR, 0, 0)
    normed, total = step(far, moments)
    normed = lax.all_to_all(normed, FAR, 0, 0)

    total, both = lax.optimization_barrier((total, both))
    basis = both.reshape(16, few + 16, half)[: rows // 8, few:].reshape(rows // 8, 2, 8, half)
    basis = basis.transpose(1, 0, 2, 3).reshape(2, rows, half)
    back_own, back_other = halves(total, core, 1)
    own_gradient = in_order(back_own, swap_cores(back_other), core, 0)
    basis = halves(basis, core, 0)
    normed, own_gradient, basis = lax.optimization_barrier((normed, own_gradient, basis))
    own_gradient = own_gradient.transpose(1, 0, 2).reshape(each // 2, rank).T
    moment_first, moment_second = adam(
        beta_first * moment_one, beta_second * moment_two, own_gradient
    )

    normed = spread(normed.reshape(16 * each, 128), NEAR, 4)
    normed = normed.reshape((2,) * 6 + (each, 128))
    order = [(NEAR + FAR).index(axis) for axis in AXES[:5]]
    normed = normed.transpose(*order, 6, 5, 7).reshape(width, half)
    basis_own, basis_other = basis
    update_other = swap_cores(contract(basis_other[0], normed, 1, 1).astype(bf16))
    update = contract(basis_own[0], normed, 1, 1) + update_other.astype(f32)
    return (update.astype(bf16), moment_first, moment_second)


def solution(mesh):
    fine = Mesh(mesh.devices.reshape(SIZES), AXES)
    placed = (
        P(DP, TENSOR),
        P(DP, TENSOR),
        P(TENSOR, None),
        P(None, TENSOR + DP),
        P(None, TENSOR + DP),
    )
    return jax.shard_map(
        local,
        mesh=fine,
        in_specs=placed,
        out_specs=(P(DP, TENSOR), P(None, TENSOR + DP), P(None, TENSOR + DP)),
        check_vma=False,
    )
```
